256 devices in a mesh: gz: 64 (over y, z, core), ma: 4 (over x).
Axes of the slice: x: 4, y: 4, z: 8, core: 2. Of those that a mesh axis runs over, the one named last changes fastest.
Arguments:
- predictor: float32 [3, 64, 512, 512], P(None, 'gz', 'ma'), may hold values from -6 to 6
- stress: float32 [6, 64, 512, 512], P(None, 'gz', 'ma'), may hold values from -6 to 6
- phase: int32 [64, 512, 512], P('gz', 'ma'), may hold values 0 or 1
- old_pressure: float32 [64, 512, 512], P('gz', 'ma'), may hold values from -6 to 6
Outputs:
- velocity: float32 [3, 64, 512, 512], P(None, 'gz', 'ma')
- pressure: float32 [64, 512, 512], P('gz', 'ma')
The draws below stay inside these ranges and needn't reach their ends.
All inputs are finite; a program needn't handle non-finite values. No bound on the sum of `phase` on one device may be relied on, other than what follows from the above.
Results may differ from the reference program's by a relative error of at most 0.0003.
Values sent between devices are 32-bit elements; how exact they have to be, the bound alone decides.
No kernel may reach another device: no remote copies, remote signals or barrier semaphores. Data moves between devices by JAX's collectives and lax.ppermute only.
A program may use at most 192 MiB of HBM per device.

```python
import jax
import jax.numpy as jnp
from jax import lax

NX = 512
NY = 512
NZ = 64


def place_ends(array, own_key, least, high):
    longest = array.shape.index(max(array.shape))
    spots = []
    for shift in (0, 1):
        where = [jax.random.randint(jax.random.fold_in(own_key, axis), (), 0, length) for axis, length in enumerate(array.shape)]
        where[longest] = (where[longest] + shift) % array.shape[longest]
        spots.append(tuple(where))
    return array.at[spots[0]].set(least).at[spots[1]].set(high)


def steps_of(rng, extent, pieces, smallest, largest):
    gain, own = 1.0, jax.random.fold_in(rng, 6)
    for position, blocks in pieces:
        draws = jnp.exp(jax.random.uniform(jax.random.fold_in(own, position), (blocks,), jnp.float32, smallest / len(pieces), largest / len(pieces)))
        gain = gain * jnp.repeat(draws, extent[position] // blocks).reshape([-1 if axis == position else 1 for axis in range(len(extent))])
    return gain


def bell_draw(key, shape, scale, bound, cuts=(), kind=jnp.bfloat16):
    drawn = scale * jax.random.normal(key, shape, jnp.float32)
    if cuts:
        drawn = drawn * steps_of(key, shape, cuts, -0.22, 0.18)
    return jnp.clip(drawn, -bound, bound).astype(kind)


def setup_inputs(seed: int = 0) -> dict:
    keys = jax.random.split(jax.random.key(seed), 5)
    predictor = bell_draw(keys[0], (3, NZ, NX, NY), 1.0, 6.0, ((1, 64), (2, 4)), jnp.float32)
    stress = bell_draw(keys[1], (6, NZ, NX, NY), 1.0, 6.0, ((1, 64), (2, 4)), jnp.float32)
    phase = place_ends((jax.random.randint(keys[2], (NZ, NX, NY), 0, 2) < 1).astype(jnp.int32), jax.random.fold_in(keys[2], 1), 0, 1)
    old_pressure = bell_draw(keys[3], (NZ, NX, NY), 1.0, 6.0, ((0, 64), (1, 4)), jnp.float32)
    return {"predictor": predictor, "stress": stress, "phase": phase, "old_pressure": old_pressure}


DENSE_LIQUID = 1.0
DENSE_GAS = 0.1
VISCOUS_LIQUID = 0.5
VISCOUS_GAS = 0.05
TIME_STEP = 0.05
SHIFT_TERM = 0.001
HIGHEST = lax.Precision.HIGHEST

def cosine_table(count):
    index = jnp.arange(count, dtype=jnp.int32)
    product = index[:, None] * (2 * index[None, :] + 1) % (4 * count)
    angle = jnp.pi * product.astype(jnp.float32) / (2.0 * count)
    weight = jnp.where(index == 0, jnp.float32((1.0 / count) ** 0.5), jnp.float32((2.0 / count) ** 0.5))
    return weight[:, None] * jnp.cos(angle)

def eigen_part(count, index):
    return 2.0 - 2.0 * jnp.cos(jnp.pi * index.astype(jnp.float32) / count)

def centred(padded, along):
    if along == 0:
        return (padded[..., 1:-1, 2:, 1:-1] - padded[..., 1:-1, :-2, 1:-1]) * 0.5
    if along == 1:
        return (padded[..., 1:-1, 1:-1, 2:] - padded[..., 1:-1, 1:-1, :-2]) * 0.5
    return (padded[..., 2:, 1:-1, 1:-1] - padded[..., :-2, 1:-1, 1:-1]) * 0.5

def laplace(padded):
    centre = padded[..., 1:-1, 1:-1, 1:-1]
    total = padded[..., 1:-1, 2:, 1:-1] + padded[..., 1:-1, :-2, 1:-1]
    total = total + padded[..., 1:-1, 1:-1, 2:] + padded[..., 1:-1, 1:-1, :-2]
    total = total + padded[..., 2:, 1:-1, 1:-1] + padded[..., :-2, 1:-1, 1:-1]
    return total - 6.0 * centre

def predict(padded, predictor, density, viscosity):
    vel_pad = padded[0:3]
    str_pad = padded[3:9]
    old_pad = padded[9]
    lap = laplace(vel_pad)
    force_x = centred(str_pad[0], 0) + centred(str_pad[3], 1) + centred(str_pad[4], 2) + viscosity * lap[0]
    force_y = centred(str_pad[3], 0) + centred(str_pad[1], 1) + centred(str_pad[5], 2) + viscosity * lap[1]
    force_z = centred(str_pad[4], 0) + centred(str_pad[5], 1) + centred(str_pad[2], 2) + viscosity * lap[2]
    force = jnp.stack([force_x, force_y, force_z])
    star = predictor + TIME_STEP / density * force
    old_gradient = jnp.stack([centred(old_pad, 0), centred(old_pad, 1), centred(old_pad, 2)])
    flux = (1.0 - DENSE_GAS / density) * old_gradient
    return (star, flux, old_gradient)

def source_of(padded):
    star_pad = padded[0:3]
    flux_pad = padded[3:6]
    div_star = centred(star_pad[0], 0) + centred(star_pad[1], 1) + centred(star_pad[2], 2)
    div_flux = centred(flux_pad[0], 0) + centred(flux_pad[1], 1) + centred(flux_pad[2], 2)
    return DENSE_GAS / TIME_STEP * div_star + div_flux

def pad_three(field):
    widths = [(0, 0)] * (field.ndim - 3) + [(1, 1), (1, 1), (1, 1)]
    return jnp.pad(field, widths)

def reference(predictor, stress, phase, old_pressure):
    liquid = phase == 1
    density = jnp.where(liquid, jnp.float32(DENSE_LIQUID), jnp.float32(DENSE_GAS))
    viscosity = jnp.where(liquid, jnp.float32(VISCOUS_LIQUID), jnp.float32(VISCOUS_GAS))
    stacked = jnp.concatenate([predictor, stress, old_pressure[None]], 0)
    star, flux, old_gradient = predict(pad_three(stacked), predictor, density, viscosity)
    source = source_of(pad_three(jnp.concatenate([star, flux], 0)))
    count_x = source.shape[1]
    count_y = source.shape[2]
    table_x = cosine_table(count_x)
    table_y = cosine_table(count_y)
    along_y = jnp.einsum('zxy,ly->zxl', source, table_y, precision=HIGHEST)
    modes = jnp.einsum('kx,zxl->zkl', table_x, along_y, precision=HIGHEST)
    spread = SHIFT_TERM + eigen_part(count_x, jnp.arange(count_x, dtype=jnp.int32))[:, None] + eigen_part(count_y, jnp.arange(count_y, dtype=jnp.int32))[None, :]
    ratio = 2.0 / (2.0 + spread + jnp.sqrt(spread * (spread + 4.0)))
    start = jnp.zeros((count_x, count_y), jnp.float32)

    def downward(carry, plane):
        carry = ratio * (carry - plane)
        return (carry, carry)
    _, lower = lax.scan(downward, start, modes)

    def upward(carry, plane):
        carry = ratio * carry + plane
        return (carry, carry)
    _, solved = lax.scan(upward, start, lower, reverse=True)
    back_x = jnp.einsum('kx,zkl->zxl', table_x, solved, precision=HIGHEST)
    pressure = jnp.einsum('zxl,ly->zxy', back_x, table_y, precision=HIGHEST)
    pres_pad = pad_three(pressure)
    gradient = jnp.stack([centred(pres_pad, 0), centred(pres_pad, 1), centred(pres_pad, 2)])
    velocity = star - TIME_STEP * (1.0 / DENSE_GAS * gradient + (1.0 / density - 1.0 / DENSE_GAS) * old_gradient)
    return (velocity, pressure)
```

```python
import jax
import jax.numpy as jnp
import numpy as np
from jax import lax
from jax.experimental import pallas as pl
from jax.experimental.pallas import tpu as pltpu
from jax.sharding import PartitionSpec as P

SHIFT_TERM = 0.001
VISCOUS = 0.025
STRESS_LIQUID = 0.025
STRESS_GAS = 0.25
OLD_LIQUID = 0.225
VMEM_LIMIT = 16 * 1024 * 1024
F32 = jnp.float32
BF16 = jnp.bfloat16


def cosine_parts(count):
    index = np.arange(count, dtype=np.int64)
    product = index[:, None] * (2 * index[None, :] + 1) % (4 * count)
    angle = np.pi * product.astype(np.float64) / (2.0 * count)
    weight = np.where(index == 0, (1.0 / count) ** 0.5, (2.0 / count) ** 0.5)
    table = (weight[:, None] * np.cos(angle)).astype(np.float32)
    high = table.astype(BF16)
    low = (table - high.astype(np.float32)).astype(BF16)
    return high, low


def eigen_parts(count):
    index = np.arange(count).astype(np.float32)
    angle = np.float32(np.pi) * index / np.float32(count)
    return np.float32(2.0) - np.float32(2.0) * np.cos(angle).astype(np.float32)


def split(value):
    high = value.astype(BF16)
    return high, (value - high.astype(F32)).astype(BF16)


def product_3(a, b, dims):
    def dot(x, y):
        return lax.dot_general(x, y, (dims, ((), ())), preferred_element_type=F32)

    return dot(a[0], b[0]) + (dot(a[0], b[1]) + dot(a[1], b[0]))


def whole():
    return pl.BlockSpec(memory_space=pltpu.VMEM)


def call(body, outs, args, flops, scratch=()):
    shapes = [jax.ShapeDtypeStruct(shape, F32) for shape in outs]
    moved = sum(a.size * a.dtype.itemsize for a in args) + sum(4 * s.size for s in shapes)
    return pl.pallas_call(
        body,
        out_shape=shapes,
        in_specs=[whole() for _ in args],
        out_specs=[whole() for _ in outs],
        scratch_shapes=list(scratch),
        cost_estimate=pl.CostEstimate(flops=flops, bytes_accessed=moved, transcendentals=0),
        compiler_params=pltpu.CompilerParams(vmem_limit_bytes=VMEM_LIMIT),
    )(*args)


def rows_body(pred, stress, old, even_row, odd_row):
    rows = old.shape[1]
    even = lax.axis_index("ma") % 2 == 0

    planes = [pred.at[i, 0] for i in range(3)] + [stress.at[i, 0] for i in (0, 3, 4)] + [old.at[0]]
    for i, plane in enumerate(planes):
        low, high = plane[0:1], plane[rows - 1 : rows]
        even_row[i : i + 1] = jnp.where(even, high, low)
        odd_row[i : i + 1] = jnp.where(even, low, high)
    even_row[7:8] = jnp.zeros_like(even_row[7:8])
    odd_row[7:8] = jnp.zeros_like(odd_row[7:8])


def send_body(pred, stress, old, far_phase, near_phase, _, far, near):
    odd = lax.axis_index("gz") % 2 == 1
    far_sign = jnp.where(odd, F32(-1), F32(1))
    for out, phase, sign in ((far, far_phase, far_sign), (near, near_phase, -far_sign)):
        liquid = phase[0] == 1
        half = jnp.where(liquid, sign * STRESS_LIQUID, sign * STRESS_GAS)
        out[0] = VISCOUS * pred[0, 0] + half * stress[4, 0]
        out[1] = VISCOUS * pred[1, 0] + half * stress[5, 0]
        push = jnp.where(liquid, sign * OLD_LIQUID, 0.0)
        out[2] = VISCOUS * pred[2, 0] + half * stress[2, 0] + push * old[0]


def shifted(value, low_row=None, high_row=None):
    rows = value.shape[0]
    spot = lax.broadcasted_iota(jnp.int32, value.shape, 0)
    low_row = F32(0) if low_row is None else low_row
    high_row = F32(0) if high_row is None else high_row
    below = jnp.where(spot == 0, low_row, pltpu.roll(value, 1, 0))
    above = jnp.where(spot == rows - 1, high_row, pltpu.roll(value, rows - 1, 0))
    return below, above


def shifted_y(value):
    columns = value.shape[1]
    spot = lax.broadcasted_iota(jnp.int32, value.shape, 1)
    below = jnp.where(spot == 0, 0.0, pltpu.roll(value, 1, 1))
    above = jnp.where(spot == columns - 1, 0.0, pltpu.roll(value, columns - 1, 1))
    return below, above


def local_body(pred, stress, phase, old, even_row, odd_row, out):
    even = lax.axis_index("ma") % 2 == 0
    before = jnp.where(even, odd_row[...], even_row[...])
    after = jnp.where(even, even_row[...], odd_row[...])
    liquid = phase[0] == 1
    half = jnp.where(liquid, STRESS_LIQUID, STRESS_GAS)

    def along_x(value, row):
        below, above = shifted(value, before[row : row + 1], after[row : row + 1])
        return above - below

    def along_y(value):
        below, above = shifted_y(value)
        return above - below

    for i in range(3):
        centre = pred[i, 0]
        below, above = shifted(centre, before[i : i + 1], after[i : i + 1])
        left, right = shifted_y(centre)
        total = centre + VISCOUS * ((below + above) + (left + right) - 6.0 * centre)
        if i == 0:
            force = along_x(stress[0, 0], 3) + along_y(stress[3, 0])
            push = along_x(old[0], 6)
        elif i == 1:
            force = along_x(stress[3, 0], 4) + along_y(stress[1, 0])
            push = along_y(old[0])
        else:
            force = along_x(stress[4, 0], 5) + along_y(stress[5, 0])
            push = None
        total = total + half * force
        if push is not None:
            total = total + jnp.where(liquid, OLD_LIQUID * push, 0.0)
        out[i] = total


def source_body(local, far, near, high, low, out, sent):
    u_x = local[0] + (far[0] + near[0])
    u_y = local[1] + (far[1] + near[1])
    u_z = local[2] + (far[2] + near[2])
    out[0], out[1], out[2] = u_x, u_y, u_z
    behind, ahead = shifted(u_x)
    left, right = shifted_y(u_y)
    planar = (ahead - behind) + (right - left)
    table = (high[...], low[...])
    nt = ((1,), (1,))
    pairs = sent.shape[0] // 5
    for i, value in enumerate((planar, u_z)):
        modes = product_3(table, split(value), nt)
        sent[pl.ds(2 * i, pairs, 5)] = modes[:pairs]
        sent[pl.ds(2 * i + 1, pairs, 5)] = modes[pairs:]
    rows, columns = u_x.shape
    first, last = u_x[0:1], u_x[rows - 1 : rows]
    spot = lax.broadcasted_iota(jnp.int32, (128, columns), 0)
    zero = jnp.zeros((128, columns), F32)
    lead = jnp.where(spot == 0, first, jnp.where(spot == 1, last, zero))
    trail = jnp.where(spot == 2, first, jnp.where(spot == 3, last, zero))
    ends = product_3((high[:pairs], low[:pairs]), split(lead), nt)
    ends = ends + product_3((high[pairs:], low[pairs:]), split(trail), nt)
    sent[pl.ds(4, pairs, 5)] = ends


def solve_body(blocks, received, ratio, high, low, sent, held, result):
    planes = received.shape[0] // (5 * blocks)
    step = 5 * blocks
    tiles = ratio.shape[0] // 2
    lane = lax.broadcasted_iota(jnp.int32, (planes, 128), 1)
    row = lax.broadcasted_iota(jnp.int32, (planes, 128), 0)
    ends = [received[pl.ds(5 * b + 4, planes, step)] for b in range(blocks)]
    sides = []
    for j in range(2):
        parts = []
        for b in range(blocks):
            source = received[pl.ds(5 * b + j, planes, step)]
            if b + 1 < blocks:
                source = source + jnp.where(lane == 127, ends[b + 1][:, 2 * j : 2 * j + 1], 0.0)
            if b > 0:
                source = source - jnp.where(lane == 0, ends[b - 1][:, 2 * j + 1 : 2 * j + 2], 0.0)
            u_z = received[pl.ds(5 * b + 2 + j, planes, step)]
            up = jnp.where(row == planes - 1, 0.0, pltpu.roll(u_z, planes - 1, 0))
            down = jnp.where(row == 0, 0.0, pltpu.roll(u_z, 1, 0))
            parts.append(source + (up - down))
        sides.append(jnp.concatenate(parts, 1))
    table = (high[...], low[...])
    modes = product_3(split(jnp.concatenate(sides, 0)), table, ((1,), (1,)))
    every = 2 * tiles
    for j in range(2):
        for t in range(tiles):
            held[pl.ds(j * tiles + t, planes, every)] = modes[
                j * planes : (j + 1) * planes, t * 128 : (t + 1) * 128
            ]
    r = ratio[...]
    carry = jnp.zeros_like(r)
    for z in range(planes):
        carry = r * (carry - held[every * z : every * (z + 1)])
        held[every * z : every * (z + 1)] = carry
    carry = jnp.zeros_like(r)
    result[0:every] = carry
    result[every * (planes + 1) : every * (planes + 2)] = carry
    for z in reversed(range(planes)):
        carry = r * carry + held[every * z : every * (z + 1)]
        result[every * (z + 1) : every * (z + 2)] = carry
    fields = []
    for j in range(2):
        pieces = [result[pl.ds(every + j * tiles + t, planes, every)] for t in range(tiles)]
        fields.append(jnp.concatenate(pieces, 1))
    for j in range(2):
        pieces = [
            result[pl.ds(2 * every + j * tiles + t, planes, every)]
            - result[pl.ds(j * tiles + t, planes, every)]
            for t in range(tiles)
        ]
        fields.append(jnp.concatenate(pieces, 1))
    back = product_3(split(jnp.concatenate(fields, 0)), table, ((1,), (0,)))
    for i in range(4):
        for b in range(blocks):
            sent[pl.ds(5 * b + i, planes, step)] = back[
                i * planes : (i + 1) * planes, b * 128 : (b + 1) * 128
            ]
    for b in range(blocks):
        edge = jnp.zeros((planes, 128), F32)
        for j in range(2):
            mine = back[j * planes : (j + 1) * planes]
            if b > 0:
                edge = jnp.where(lane == 2 * j, mine[:, b * 128 - 1 : b * 128], edge)
            if b + 1 < blocks:
                edge = jnp.where(
                    lane == 2 * j + 1, mine[:, b * 128 + 128 : b * 128 + 129], edge
                )
        sent[pl.ds(5 * b + 4, planes, step)] = edge


def final_body(received, u, high, low, velocity, pressure):
    pairs = received.shape[0] // 5
    table = (high[...], low[...])
    nn = ((1,), (0,))

    def field(i):
        pieces = [received[pl.ds(i + j, pairs, 5)] for j in range(2)]
        return product_3(split(jnp.concatenate(pieces, 0).T), table, nn)

    p = field(0)
    along_z = field(2)
    ends = split(received[pl.ds(4, pairs, 5)].T[0:8])
    lead = product_3(ends, (high[:pairs], low[:pairs]), nn)
    trail = product_3(ends, (high[pairs:], low[pairs:]), nn)
    behind, ahead = shifted(p, lead[0:1] + trail[2:3], lead[1:2] + trail[3:4])
    left, right = shifted_y(p)
    pressure[0] = p
    velocity[0, 0] = u[0] - 0.25 * (ahead - behind)
    velocity[1, 0] = u[1] - 0.25 * (right - left)
    velocity[2, 0] = u[2] - 0.25 * along_z


def shards(predictor, stress, phase, old_pressure):
    planes_z, lines = lax.axis_size("gz"), lax.axis_size("ma")
    rows, columns = old_pressure.shape[1], old_pressure.shape[2]
    devices = planes_z * lines
    table = cosine_parts(columns)
    high, low = jnp.asarray(table[0]), jnp.asarray(table[1])
    eigen = eigen_parts(columns)

    def swap(value, axis, begin):
        pairs = [(i, i + 1) for i in range(begin, lax.axis_size(axis) - 1, 2)]
        return lax.ppermute(value, axis, pairs + [(b, a) for a, b in pairs])

    far_phase = swap(phase, "gz", 1)
    near_phase = swap(phase, "gz", 0)
    even_row, odd_row = call(
        rows_body, [(8, columns), (8, columns)], (predictor, stress, old_pressure), 10000
    )
    far, near = call(
        send_body,
        [(3, rows, columns), (3, rows, columns)],
        (predictor, stress, old_pressure, far_phase, near_phase, even_row),
        1000000,
    )
    even_row = swap(even_row, "ma", 0)
    odd_row = swap(odd_row, "ma", 1)
    far = swap(far, "gz", 1)
    near = swap(near, "gz", 0)

    own = lax.axis_index("gz") * lines + lax.axis_index("ma")
    tiles = columns // 128
    part_x = jnp.asarray(np.tile(eigen.reshape(tiles, 128), (2, 1)))
    pair = lax.dynamic_index_in_dim(
        jnp.asarray(eigen.reshape(2, devices)), own, 1, keepdims=False
    )
    part_y = jnp.repeat(pair, tiles)[:, None]
    spread = SHIFT_TERM + part_x + part_y
    ratio = 2.0 / (2.0 + spread + jnp.sqrt(spread * (spread + 4.0)))

    (local,) = call(
        local_body,
        [(3, rows, columns)],
        (predictor, stress, phase, old_pressure, even_row, odd_row),
        8000000,
    )
    u, modes = call(
        source_body,
        [(3, rows, columns), (5 * devices, 128)],
        (local, far, near, high, low),
        600000000,
    )

    def exchange(value):
        moved = lax.all_to_all(value.reshape(5 * devices, 1, 128), ("gz", "ma"), 0, 0, tiled=True)
        return moved.reshape(5 * devices, 128)

    (solved,) = call(
        lambda *refs: solve_body(lines, *refs),
        [(5 * devices, 128)],
        (exchange(modes), ratio, high, low),
        700000000,
        (
            pltpu.VMEM((2 * tiles * planes_z, 128), F32),
            pltpu.VMEM((2 * tiles * (planes_z + 2), 128), F32),
        ),
    )
    velocity, pressure = call(
        final_body,
        [(3, 1, rows, columns), (1, rows, columns)],
        (exchange(solved), u, high, low),
        500000000,
    )
    return velocity, pressure


def solution(mesh):
    return jax.shard_map(
        shards,
        mesh=mesh,
        in_specs=(
            P(None, "gz", "ma", None),
            P(None, "gz", "ma", None),
            P("gz", "ma", None),
            P("gz", "ma", None),
        ),
        out_specs=(P(None, "gz", "ma", None), P("gz", "ma", None)),
        check_vma=False,
    )
```

```python
import jax
import jax.numpy as jnp
import numpy as np
from jax import lax
from jax.experimental import pallas as pl
from jax.experimental.pallas import tpu as pltpu
from jax.sharding import PartitionSpec as P

SHIFT_TERM = 0.001
VISCOUS = 0.025
STRESS_LIQUID = 0.025
STRESS_GAS = 0.25
OLD_LIQUID = 0.225
VMEM_LIMIT = 16 * 1024 * 1024
F32 = jnp.float32
BF16 = jnp.bfloat16


def cosine_parts(count):
    index = np.arange(count, dtype=np.int64)
    product = index[:, None] * (2 * index[None, :] + 1) % (4 * count)
    angle = np.pi * product.astype(np.float64) / (2.0 * count)
    weight = np.where(index == 0, (1.0 / count) ** 0.5, (2.0 / count) ** 0.5)
    table = (weight[:, None] * np.cos(angle)).astype(np.float32)
    high = table.astype(BF16)
    low = (table - high.astype(np.float32)).astype(BF16)
    return high, low


def eigen_parts(count):
    index = np.arange(count).astype(np.float32)
    angle = np.float32(np.pi) * index / np.float32(count)
    return np.float32(2.0) - np.float32(2.0) * np.cos(angle).astype(np.float32)


def split(value):
    high = value.astype(BF16)
    return high, (value - high.astype(F32)).astype(BF16)


def product_3(a, b, dims):
    def dot(x, y):
        return lax.dot_general(x, y, (dims, ((), ())), preferred_element_type=F32)

    return dot(a[0], b[0]) + (dot(a[0], b[1]) + dot(a[1], b[0]))


def whole():
    return pl.BlockSpec(memory_space=pltpu.VMEM)


def call(body, outs, args, flops, scratch=(), out_space=pltpu.VMEM):
    shapes = [jax.ShapeDtypeStruct(shape, F32) for shape in outs]
    moved = sum(a.size * a.dtype.itemsize for a in args) + sum(4 * s.size for s in shapes)
    return pl.pallas_call(
        body,
        out_shape=shapes,
        in_specs=[whole() for _ in args],
        out_specs=[pl.BlockSpec(memory_space=out_space) for _ in outs],
        scratch_shapes=list(scratch),
        cost_estimate=pl.CostEstimate(flops=flops, bytes_accessed=moved, transcendentals=0),
        compiler_params=pltpu.CompilerParams(vmem_limit_bytes=VMEM_LIMIT),
    )(*args)


def near_sign():
    return jnp.where(lax.axis_index("gz") % 2 == 1, F32(1), F32(-1))


def rows_body(pred, stress, old, even_row, odd_row):
    rows = old.shape[1]
    even = lax.axis_index("ma") % 2 == 0

    planes = [pred.at[i, 0] for i in range(3)] + [stress.at[i, 0] for i in (0, 3, 4)] + [old.at[0]]
    for i, plane in enumerate(planes):
        low, high = plane[0:1], plane[rows - 1 : rows]
        even_row[i : i + 1] = jnp.where(even, high, low)
        odd_row[i : i + 1] = jnp.where(even, low, high)
    even_row[7:8] = jnp.zeros_like(even_row[7:8])
    odd_row[7:8] = jnp.zeros_like(odd_row[7:8])


def shifted(value, low_row=None, high_row=None):
    rows = value.shape[0]
    spot = lax.broadcasted_iota(jnp.int32, value.shape, 0)
    low_row = F32(0) if low_row is None else low_row
    high_row = F32(0) if high_row is None else high_row
    below = jnp.where(spot == 0, low_row, pltpu.roll(value, 1, 0))
    above = jnp.where(spot == rows - 1, high_row, pltpu.roll(value, rows - 1, 0))
    return below, above


def shifted_y(value):
    columns = value.shape[1]
    spot = lax.broadcasted_iota(jnp.int32, value.shape, 1)
    below = jnp.where(spot == 0, 0.0, pltpu.roll(value, 1, 1))
    above = jnp.where(spot == columns - 1, 0.0, pltpu.roll(value, columns - 1, 1))
    return below, above


def for_far(pred, stress, phase):
    sign = -near_sign()
    half = jnp.where(phase[0] == 1, sign * STRESS_LIQUID, sign * STRESS_GAS)
    add_x = VISCOUS * pred[0, 0] + half * stress[4, 0]
    return add_x, VISCOUS * pred[1, 0] + half * stress[5, 0]


def send_body(pred, stress, old, phase, _, far, near):
    rows = old.shape[1]
    sign = -near_sign()
    add_x, add_y = for_far(pred, stress, phase)
    behind, ahead = shifted(add_x)
    left, right = shifted_y(add_y)
    far[0:rows] = (ahead - behind) + (right - left)
    liquid = sign * (STRESS_LIQUID * stress[2, 0] + OLD_LIQUID * old[0])
    gas = (sign * STRESS_GAS) * stress[2, 0]
    viscous = VISCOUS * pred[2, 0]
    far[rows : 2 * rows] = viscous + jnp.where(phase[0] == 1, liquid, gas)
    far[2 * rows : 2 * rows + 1] = add_x[0:1]
    far[2 * rows + 1 : 2 * rows + 2] = add_x[rows - 1 : rows]
    far[2 * rows + 2 : 2 * rows + 8] = jnp.zeros((6, old.shape[2]), F32)
    near[0] = VISCOUS * pred[0, 0]
    near[1] = -sign * stress[4, 0]
    near[2] = VISCOUS * pred[1, 0]
    near[3] = -sign * stress[5, 0]
    near[4] = viscous - liquid
    near[5] = viscous - gas


def local_body(pred, stress, phase, old, even_row, odd_row, far_phase, out, later):
    later[0], later[1] = for_far(pred, stress, far_phase)
    even = lax.axis_index("ma") % 2 == 0
    before = jnp.where(even, odd_row[...], even_row[...])
    after = jnp.where(even, even_row[...], odd_row[...])
    liquid = phase[0] == 1
    half = jnp.where(liquid, STRESS_LIQUID, STRESS_GAS)

    def along_x(value, row):
        below, above = shifted(value, before[row : row + 1], after[row : row + 1])
        return above - below

    def along_y(value):
        below, above = shifted_y(value)
        return above - below

    for i in range(3):
        centre = pred[i, 0]
        below, above = shifted(centre, before[i : i + 1], after[i : i + 1])
        left, right = shifted_y(centre)
        total = centre + VISCOUS * ((below + above) + (left + right) - 6.0 * centre)
        if i == 0:
            force = along_x(stress[0, 0], 3) + along_y(stress[3, 0])
            push = along_x(old[0], 6)
        elif i == 1:
            force = along_x(stress[3, 0], 4) + along_y(stress[1, 0])
            push = along_y(old[0])
        else:
            force = along_x(stress[4, 0], 5) + along_y(stress[5, 0])
            push = None
        total = total + half * force
        if push is not None:
            total = total + jnp.where(liquid, OLD_LIQUID * push, 0.0)
        out[i] = total


def source_body(local, far, near, phase, high, low, out, sent):
    liquid = phase[0] == 1
    half = jnp.where(liquid, STRESS_LIQUID, STRESS_GAS)
    rows = local.shape[1]
    u_x = local[0] + (near[0] + half * near[1])
    u_y = local[1] + (near[2] + half * near[3])
    u_z = local[2] + far[rows : 2 * rows] + jnp.where(liquid, near[4], near[5])
    out[0], out[1], out[2] = u_x, u_y, u_z
    behind, ahead = shifted(u_x)
    left, right = shifted_y(u_y)
    planar = (ahead - behind) + (right - left) + far[0:rows]
    spot = lax.broadcasted_iota(jnp.int32, u_x.shape, 0)
    first = u_x[0:1] + far[2 * rows : 2 * rows + 1]
    last = u_x[rows - 1 : rows] + far[2 * rows + 1 : 2 * rows + 2]
    ends = jnp.where(spot == 0, first, jnp.where(spot == 1, last, 0.0))
    fields = split(jnp.concatenate([planar, u_z, ends], 0))
    modes = product_3((high[...], low[...]), fields, ((1,), (1,)))
    pairs = sent.shape[0] // 5
    for i in range(2):
        for j in range(2):
            sent[pl.ds(2 * i + j, pairs, 5)] = modes[
                j * pairs : (j + 1) * pairs, i * rows : (i + 1) * rows
            ]
    ends = modes[:, 2 * rows : 3 * rows]
    sent[pl.ds(4, pairs, 5)] = ends[:pairs] + pltpu.roll(ends[pairs:], 2, 1)


def solve_body(blocks, received, part_x, part_y, high, low, sent, held, result):
    planes = received.shape[0] // (5 * blocks)
    step = 5 * blocks
    tiles = part_x.shape[0] // 2
    lane = lax.broadcasted_iota(jnp.int32, (planes, 128), 1)
    row = lax.broadcasted_iota(jnp.int32, (planes, 128), 0)
    own = lax.axis_index("gz") * blocks + lax.axis_index("ma")
    mine = lax.broadcasted_iota(jnp.int32, part_y.shape, 1) == own
    wave_y = jnp.sum(jnp.where(mine, part_y[...], 0.0), axis=1, keepdims=True)
    spread = SHIFT_TERM + part_x[...] + wave_y
    r = 2.0 / (2.0 + spread + jnp.sqrt(spread * (spread + 4.0)))
    ends = [received[pl.ds(5 * b + 4, planes, step)] for b in range(blocks)]
    sides = []
    for j in range(2):
        parts = []
        for b in range(blocks):
            source = received[pl.ds(5 * b + j, planes, step)]
            if b + 1 < blocks:
                source = source + jnp.where(lane == 127, ends[b + 1][:, 2 * j : 2 * j + 1], 0.0)
            if b > 0:
                source = source - jnp.where(lane == 0, ends[b - 1][:, 2 * j + 1 : 2 * j + 2], 0.0)
            u_z = received[pl.ds(5 * b + 2 + j, planes, step)]
            up = jnp.where(row == planes - 1, 0.0, pltpu.roll(u_z, planes - 1, 0))
            down = jnp.where(row == 0, 0.0, pltpu.roll(u_z, 1, 0))
            parts.append(source + (up - down))
        sides.append(jnp.concatenate(parts, 1))
    table = (high[...], low[...])
    modes = product_3(split(jnp.concatenate(sides, 0)), table, ((1,), (1,)))
    every = 2 * tiles
    for j in range(2):
        for t in range(tiles):
            held[pl.ds(j * tiles + t, planes, every)] = modes[
                j * planes : (j + 1) * planes, t * 128 : (t + 1) * 128
            ]
    carry = jnp.zeros_like(r)
    for z in range(planes):
        carry = r * (carry - held[every * z : every * (z + 1)])
        held[every * z : every * (z + 1)] = carry
    carry = jnp.zeros_like(r)
    result[0:every] = carry
    result[every * (planes + 1) : every * (planes + 2)] = carry
    for z in reversed(range(planes)):
        carry = r * carry + held[every * z : every * (z + 1)]
        result[every * (z + 1) : every * (z + 2)] = carry
    fields = []
    for j in range(2):
        pieces = [result[pl.ds(every + j * tiles + t, planes, every)] for t in range(tiles)]
        fields.append(jnp.concatenate(pieces, 1))
    for j in range(2):
        pieces = [
            result[pl.ds(2 * every + j * tiles + t, planes, every)]
            - result[pl.ds(j * tiles + t, planes, every)]
            for t in range(tiles)
        ]
        fields.append(jnp.concatenate(pieces, 1))
    back = product_3(split(jnp.concatenate(fields, 0)), table, ((1,), (0,)))
    for i in range(4):
        for b in range(blocks):
            sent[pl.ds(5 * b + i, planes, step)] = back[
                i * planes : (i + 1) * planes, b * 128 : (b + 1) * 128
            ]
    for b in range(blocks):
        edge = jnp.zeros((planes, 128), F32)
        for j in range(2):
            mine = back[j * planes : (j + 1) * planes]
            if b > 0:
                edge = jnp.where(lane == 2 * j, mine[:, b * 128 - 1 : b * 128], edge)
            if b + 1 < blocks:
                edge = jnp.where(
                    lane == 2 * j + 1, mine[:, b * 128 + 128 : b * 128 + 129], edge
                )
        sent[pl.ds(5 * b + 4, planes, step)] = edge


def final_body(received, u, later, high, low, velocity, pressure, made, arrived):
    pairs = received.shape[0] // 5
    table = (high[...], low[...])
    nn = ((1,), (0,))
    places = (velocity.at[0, 0], velocity.at[1, 0], velocity.at[2, 0], pressure.at[0])
    copies = [pltpu.make_async_copy(made.at[i], places[i], arrived.at[i]) for i in range(4)]

    def field(i):
        pieces = [received[pl.ds(i + j, pairs, 5)] for j in range(2)]
        return product_3(split(jnp.concatenate(pieces, 0).T), table, nn)

    made[2] = u[2] - 0.25 * field(2)
    copies[2].start()
    p = field(0)
    made[3] = p
    copies[3].start()
    left, right = shifted_y(p)
    made[1] = u[1] + later[1] - 0.25 * (right - left)
    copies[1].start()
    ends = split(received[pl.ds(4, pairs, 5)].T[0:8])
    lead = product_3(ends, (high[:pairs], low[:pairs]), nn)
    trail = product_3(ends, (high[pairs:], low[pairs:]), nn)
    behind, ahead = shifted(p, lead[0:1] + trail[2:3], lead[1:2] + trail[3:4])
    made[0] = u[0] + later[0] - 0.25 * (ahead - behind)
    copies[0].start()
    for copy in copies:
        copy.wait()


def shards(predictor, stress, phase, old_pressure):
    planes_z, lines = lax.axis_size("gz"), lax.axis_size("ma")
    rows, columns = old_pressure.shape[1], old_pressure.shape[2]
    devices = planes_z * lines
    table = cosine_parts(columns)
    high, low = jnp.asarray(table[0]), jnp.asarray(table[1])
    eigen = eigen_parts(columns)

    def swap(value, axis, begin):
        pairs = [(i, i + 1) for i in range(begin, lax.axis_size(axis) - 1, 2)]
        return lax.ppermute(value, axis, pairs + [(b, a) for a, b in pairs])

    far_phase = swap(phase, "gz", 1)
    even_row, odd_row = call(
        rows_body, [(8, columns), (8, columns)], (predictor, stress, old_pressure), 10000
    )
    far, near = call(
        send_body,
        [(2 * rows + 8, columns), (6, rows, columns)],
        (predictor, stress, old_pressure, far_phase, even_row),
        1000000,
    )
    far = swap(far, "gz", 1)
    near = swap(near, "gz", 0)
    even_row = swap(even_row, "ma", 0)
    odd_row = swap(odd_row, "ma", 1)

    local, later = call(
        local_body,
        [(3, rows, columns), (2, rows, columns)],
        (predictor, stress, phase, old_pressure, even_row, odd_row, far_phase),
        8000000,
    )
    later = swap(later, "gz", 1)
    u, modes = call(
        source_body,
        [(3, rows, columns), (5 * devices, 128)],
        (local, far, near, phase, high, low),
        600000000,
    )

    def exchange(value):
        count = value.shape[0]
        moved = lax.all_to_all(value.reshape(count, 1, 128), ("gz", "ma"), 0, 0, tiled=True)
        return moved.reshape(count, 128)

    tiles = columns // 128
    part_x = jnp.asarray(np.tile(eigen.reshape(tiles, 128), (2, 1)))
    part_y = jnp.asarray(np.repeat(eigen.reshape(2, devices), tiles, axis=0))
    (solved,) = call(
        lambda *refs: solve_body(lines, *refs),
        [(5 * devices, 128)],
        (exchange(modes), part_x, part_y, high, low),
        700000000,
        (
            pltpu.VMEM((2 * tiles * planes_z, 128), F32),
            pltpu.VMEM((2 * tiles * (planes_z + 2), 128), F32),
        ),
    )
    velocity, pressure = call(
        final_body,
        [(3, 1, rows, columns), (1, rows, columns)],
        (exchange(solved), u, later, high, low),
        500000000,
        (pltpu.VMEM((4, rows, columns), F32), pltpu.SemaphoreType.DMA((4,))),
        pl.ANY,
    )
    return velocity, pressure


def solution(mesh):
    return jax.shard_map(
        shards,
        mesh=mesh,
        in_specs=(
            P(None, "gz", "ma", None),
            P(None, "gz", "ma", None),
            P("gz", "ma", None),
            P("gz", "ma", None),
        ),
        out_specs=(P(None, "gz", "ma", None), P("gz", "ma", None)),
        check_vma=False,
    )
```

```python
import jax
import jax.numpy as jnp
import numpy as np
from jax import lax
from jax.experimental import pallas as pl
from jax.experimental.pallas import tpu as pltpu
from jax.sharding import PartitionSpec as P

SHIFT_TERM = 0.001
VISCOUS = 0.025
STRESS_LIQUID = 0.025
STRESS_GAS = 0.25
OLD_LIQUID = 0.225
VMEM_LIMIT = 16 * 1024 * 1024
F32 = jnp.float32
BF16 = jnp.bfloat16


def cosine_parts(count):
    index = np.arange(count, dtype=np.int64)
    product = index[:, None] * (2 * index[None, :] + 1) % (4 * count)
    angle = np.pi * product.astype(np.float64) / (2.0 * count)
    weight = np.where(index == 0, (1.0 / count) ** 0.5, (2.0 / count) ** 0.5)
    table = (weight[:, None] * np.cos(angle)).astype(np.float32)
    high = table.astype(BF16)
    low = (table - high.astype(np.float32)).astype(BF16)
    return high, low


def eigen_parts(count):
    index = np.arange(count).astype(np.float32)
    angle = np.float32(np.pi) * index / np.float32(count)
    return np.float32(2.0) - np.float32(2.0) * np.cos(angle).astype(np.float32)


def split(value):
    high = value.astype(BF16)
    return high, (value - high.astype(F32)).astype(BF16)


def product_3(a, b, dims):
    def dot(x, y):
        return lax.dot_general(x, y, (dims, ((), ())), preferred_element_type=F32)

    return dot(a[0], b[0]) + (dot(a[0], b[1]) + dot(a[1], b[0]))


def whole():
    return pl.BlockSpec(memory_space=pltpu.VMEM)


def call(body, outs, args, flops, scratch=(), out_space=pltpu.VMEM):
    shapes = [jax.ShapeDtypeStruct(shape, F32) for shape in outs]
    moved = sum(a.size * a.dtype.itemsize for a in args) + sum(4 * s.size for s in shapes)
    return pl.pallas_call(
        body,
        out_shape=shapes,
        in_specs=[whole() for _ in args],
        out_specs=[pl.BlockSpec(memory_space=out_space) for _ in outs],
        scratch_shapes=list(scratch),
        cost_estimate=pl.CostEstimate(flops=flops, bytes_accessed=moved, transcendentals=0),
        compiler_params=pltpu.CompilerParams(vmem_limit_bytes=VMEM_LIMIT),
    )(*args)


def near_sign():
    return jnp.where(lax.axis_index("gz") % 2 == 1, F32(1), F32(-1))


def rows_body(pred, stress, old, even_row, odd_row):
    rows = old.shape[1]
    even = lax.axis_index("ma") % 2 == 0

    planes = [pred.at[i, 0] for i in range(3)] + [stress.at[i, 0] for i in (0, 3, 4)] + [old.at[0]]
    for i, plane in enumerate(planes):
        low, high = plane[0:1], plane[rows - 1 : rows]
        even_row[i : i + 1] = jnp.where(even, high, low)
        odd_row[i : i + 1] = jnp.where(even, low, high)
    even_row[7:8] = jnp.zeros_like(even_row[7:8])
    odd_row[7:8] = jnp.zeros_like(odd_row[7:8])


def shifted(value, low_row=None, high_row=None):
    rows = value.shape[0]
    spot = lax.broadcasted_iota(jnp.int32, value.shape, 0)
    low_row = F32(0) if low_row is None else low_row
    high_row = F32(0) if high_row is None else high_row
    below = jnp.where(spot == 0, low_row, pltpu.roll(value, 1, 0))
    above = jnp.where(spot == rows - 1, high_row, pltpu.roll(value, rows - 1, 0))
    return below, above


def shifted_y(value):
    columns = value.shape[1]
    spot = lax.broadcasted_iota(jnp.int32, value.shape, 1)
    below = jnp.where(spot == 0, 0.0, pltpu.roll(value, 1, 1))
    above = jnp.where(spot == columns - 1, 0.0, pltpu.roll(value, columns - 1, 1))
    return below, above


def for_far(pred, stress, phase):
    sign = -near_sign()
    half = jnp.where(phase[0] == 1, sign * STRESS_LIQUID, sign * STRESS_GAS)
    add_x = VISCOUS * pred[0, 0] + half * stress[4, 0]
    return add_x, VISCOUS * pred[1, 0] + half * stress[5, 0]


def send_body(pred, stress, old, phase, _, far, near):
    rows = old.shape[1]
    sign = -near_sign()
    add_x, add_y = for_far(pred, stress, phase)
    behind, ahead = shifted(add_x)
    left, right = shifted_y(add_y)
    far[0:rows] = (ahead - behind) + (right - left)
    liquid = sign * (STRESS_LIQUID * stress[2, 0] + OLD_LIQUID * old[0])
    gas = (sign * STRESS_GAS) * stress[2, 0]
    viscous = VISCOUS * pred[2, 0]
    far[rows : 2 * rows] = viscous + jnp.where(phase[0] == 1, liquid, gas)
    far[2 * rows : 2 * rows + 1] = add_x[0:1]
    far[2 * rows + 1 : 2 * rows + 2] = add_x[rows - 1 : rows]
    far[2 * rows + 2 : 2 * rows + 8] = jnp.zeros((6, old.shape[2]), F32)
    near[0] = VISCOUS * pred[0, 0]
    near[1] = -sign * stress[4, 0]
    near[2] = VISCOUS * pred[1, 0]
    near[3] = -sign * stress[5, 0]
    near[4] = viscous - liquid
    near[5] = viscous - gas


def local_body(pred, stress, phase, old, even_row, odd_row, far_phase, out, later):
    later[0], later[1] = for_far(pred, stress, far_phase)
    even = lax.axis_index("ma") % 2 == 0
    before = jnp.where(even, odd_row[...], even_row[...])
    after = jnp.where(even, even_row[...], odd_row[...])
    liquid = phase[0] == 1
    half = jnp.where(liquid, STRESS_LIQUID, STRESS_GAS)

    def along_x(value, row):
        below, above = shifted(value, before[row : row + 1], after[row : row + 1])
        return above - below

    def along_y(value):
        below, above = shifted_y(value)
        return above - below

    for i in range(3):
        centre = pred[i, 0]
        below, above = shifted(centre, before[i : i + 1], after[i : i + 1])
        left, right = shifted_y(centre)
        total = centre + VISCOUS * ((below + above) + (left + right) - 6.0 * centre)
        if i == 0:
            force = along_x(stress[0, 0], 3) + along_y(stress[3, 0])
            push = along_x(old[0], 6)
        elif i == 1:
            force = along_x(stress[3, 0], 4) + along_y(stress[1, 0])
            push = along_y(old[0])
        else:
            force = along_x(stress[4, 0], 5) + along_y(stress[5, 0])
            push = None
        total = total + half * force
        if push is not None:
            total = total + jnp.where(liquid, OLD_LIQUID * push, 0.0)
        out[i] = total


def source_body(local, far, near, phase, high, low, out, sent):
    liquid = phase[0] == 1
    half = jnp.where(liquid, STRESS_LIQUID, STRESS_GAS)
    rows = local.shape[1]
    u_x = local[0] + (near[0] + half * near[1])
    u_y = local[1] + (near[2] + half * near[3])
    u_z = local[2] + far[rows : 2 * rows] + jnp.where(liquid, near[4], near[5])
    out[0], out[1], out[2] = u_x, u_y, u_z
    behind, ahead = shifted(u_x)
    left, right = shifted_y(u_y)
    planar = (ahead - behind) + (right - left) + far[0:rows]
    spot = lax.broadcasted_iota(jnp.int32, u_x.shape, 0)
    first = u_x[0:1] + far[2 * rows : 2 * rows + 1]
    last = u_x[rows - 1 : rows] + far[2 * rows + 1 : 2 * rows + 2]
    ends = jnp.where(spot == 0, first, jnp.where(spot == 1, last, 0.0))
    fields = split(jnp.concatenate([planar, u_z, ends], 0))
    modes = product_3((high[...], low[...]), fields, ((1,), (1,)))
    pairs = sent.shape[0] // 5
    for i in range(2):
        for j in range(2):
            sent[pl.ds(2 * i + j, pairs, 5)] = modes[
                j * pairs : (j + 1) * pairs, i * rows : (i + 1) * rows
            ]
    ends = modes[:, 2 * rows : 3 * rows]
    sent[pl.ds(4, pairs, 5)] = ends[:pairs] + pltpu.roll(ends[pairs:], 2, 1)


def solve_body(blocks, received, part_x, part_y, high, low, sent, held, result):
    planes = received.shape[0] // (5 * blocks)
    step = 5 * blocks
    tiles = part_x.shape[0] // 2
    lane = lax.broadcasted_iota(jnp.int32, (planes, 128), 1)
    row = lax.broadcasted_iota(jnp.int32, (planes, 128), 0)
    own = lax.axis_index("gz") * blocks + lax.axis_index("ma")
    mine = lax.broadcasted_iota(jnp.int32, part_y.shape, 1) == own
    wave_y = jnp.sum(jnp.where(mine, part_y[...], 0.0), axis=1, keepdims=True)
    spread = SHIFT_TERM + part_x[...] + wave_y
    r = 2.0 / (2.0 + spread + jnp.sqrt(spread * (spread + 4.0)))
    ends = [received[pl.ds(5 * b + 4, planes, step)] for b in range(blocks)]
    sides = []
    for j in range(2):
        parts = []
        for b in range(blocks):
            source = received[pl.ds(5 * b + j, planes, step)]
            if b + 1 < blocks:
                source = source + jnp.where(lane == 127, ends[b + 1][:, 2 * j : 2 * j + 1], 0.0)
            if b > 0:
                source = source - jnp.where(lane == 0, ends[b - 1][:, 2 * j + 1 : 2 * j + 2], 0.0)
            u_z = received[pl.ds(5 * b + 2 + j, planes, step)]
            up = jnp.where(row == planes - 1, 0.0, pltpu.roll(u_z, planes - 1, 0))
            down = jnp.where(row == 0, 0.0, pltpu.roll(u_z, 1, 0))
            parts.append(source + (up - down))
        sides.append(jnp.concatenate(parts, 1))
    table = (high[...], low[...])
    modes = product_3(split(jnp.concatenate(sides, 0)), table, ((1,), (1,)))
    every = 2 * tiles
    for j in range(2):
        for t in range(tiles):
            held[pl.ds(j * tiles + t, planes, every)] = modes[
                j * planes : (j + 1) * planes, t * 128 : (t + 1) * 128
            ]
    half = planes // 2
    zero = jnp.zeros_like(r)
    powers = [r]
    for _ in range(half - 1):
        powers.append(powers[-1] * r)
    carry, other = zero, zero
    for z in range(half):
        here = slice(every * z, every * (z + 1))
        there = slice(every * (z + half), every * (z + half + 1))
        carry = r * (carry - held[here])
        other = r * (other - held[there])
        held[here] = carry
        held[there] = other
    for z in range(half):
        there = slice(every * (z + half), every * (z + half + 1))
        held[there] = held[there] + powers[z] * carry
    result[0:every] = zero
    result[every * (planes + 1) : every * (planes + 2)] = zero
    carry, other = zero, zero
    for z in range(half):
        low, high_z = half - 1 - z, planes - 1 - z
        carry = r * carry + held[every * high_z : every * (high_z + 1)]
        other = r * other + held[every * low : every * (low + 1)]
        result[every * (high_z + 1) : every * (high_z + 2)] = carry
        result[every * (low + 1) : every * (low + 2)] = other
    for z in range(half):
        here = slice(every * (half - z), every * (half - z + 1))
        result[here] = result[here] + powers[z] * carry
    fields = []
    for j in range(2):
        pieces = [result[pl.ds(every + j * tiles + t, planes, every)] for t in range(tiles)]
        fields.append(jnp.concatenate(pieces, 1))
    for j in range(2):
        pieces = [
            result[pl.ds(2 * every + j * tiles + t, planes, every)]
            - result[pl.ds(j * tiles + t, planes, every)]
            for t in range(tiles)
        ]
        fields.append(jnp.concatenate(pieces, 1))
    back = product_3(split(jnp.concatenate(fields, 0)), table, ((1,), (0,)))
    for i in range(4):
        for b in range(blocks):
            sent[pl.ds(5 * b + i, planes, step)] = back[
                i * planes : (i + 1) * planes, b * 128 : (b + 1) * 128
            ]
    for b in range(blocks):
        edge = jnp.zeros((planes, 128), F32)
        for j in range(2):
            mine = back[j * planes : (j + 1) * planes]
            if b > 0:
                edge = jnp.where(lane == 2 * j, mine[:, b * 128 - 1 : b * 128], edge)
            if b + 1 < blocks:
                edge = jnp.where(
                    lane == 2 * j + 1, mine[:, b * 128 + 128 : b * 128 + 129], edge
                )
        sent[pl.ds(5 * b + 4, planes, step)] = edge


def final_body(received, u, later, high, low, velocity, pressure, made, arrived):
    pairs = received.shape[0] // 5
    table = (high[...], low[...])
    nn = ((1,), (0,))
    places = (velocity.at[0, 0], velocity.at[1, 0], velocity.at[2, 0], pressure.at[0])
    copies = [pltpu.make_async_copy(made.at[i], places[i], arrived.at[i]) for i in range(4)]

    def field(i):
        pieces = [received[pl.ds(i + j, pairs, 5)] for j in range(2)]
        return product_3(split(jnp.concatenate(pieces, 0).T), table, nn)

    made[2] = u[2] - 0.25 * field(2)
    copies[2].start()
    p = field(0)
    made[3] = p
    copies[3].start()
    left, right = shifted_y(p)
    made[1] = u[1] + later[1] - 0.25 * (right - left)
    copies[1].start()
    ends = split(received[pl.ds(4, pairs, 5)].T[0:8])
    lead = product_3(ends, (high[:pairs], low[:pairs]), nn)
    trail = product_3(ends, (high[pairs:], low[pairs:]), nn)
    behind, ahead = shifted(p, lead[0:1] + trail[2:3], lead[1:2] + trail[3:4])
    made[0] = u[0] + later[0] - 0.25 * (ahead - behind)
    copies[0].start()
    for copy in copies:
        copy.wait()


def shards(predictor, stress, phase, old_pressure):
    planes_z, lines = lax.axis_size("gz"), lax.axis_size("ma")
    rows, columns = old_pressure.shape[1], old_pressure.shape[2]
    devices = planes_z * lines
    table = cosine_parts(columns)
    high, low = jnp.asarray(table[0]), jnp.asarray(table[1])
    eigen = eigen_parts(columns)

    def swap(value, axis, begin):
        pairs = [(i, i + 1) for i in range(begin, lax.axis_size(axis) - 1, 2)]
        return lax.ppermute(value, axis, pairs + [(b, a) for a, b in pairs])

    far_phase = swap(phase, "gz", 1)
    even_row, odd_row = call(
        rows_body, [(8, columns), (8, columns)], (predictor, stress, old_pressure), 10000
    )
    far, near = call(
        send_body,
        [(2 * rows + 8, columns), (6, rows, columns)],
        (predictor, stress, old_pressure, far_phase, even_row),
        1000000,
    )
    far = swap(far, "gz", 1)
    near = swap(near, "gz", 0)
    even_row = swap(even_row, "ma", 0)
    odd_row = swap(odd_row, "ma", 1)

    local, later = call(
        local_body,
        [(3, rows, columns), (2, rows, columns)],
        (predictor, stress, phase, old_pressure, even_row, odd_row, far_phase),
        8000000,
    )
    later = swap(later, "gz", 1)
    u, modes = call(
        source_body,
        [(3, rows, columns), (5 * devices, 128)],
        (local, far, near, phase, high, low),
        600000000,
    )

    def exchange(value):
        count = value.shape[0]
        moved = lax.all_to_all(value.reshape(count, 1, 128), ("gz", "ma"), 0, 0, tiled=True)
        return moved.reshape(count, 128)

    tiles = columns // 128
    part_x = jnp.asarray(np.tile(eigen.reshape(tiles, 128), (2, 1)))
    part_y = jnp.asarray(np.repeat(eigen.reshape(2, devices), tiles, axis=0))
    (solved,) = call(
        lambda *refs: solve_body(lines, *refs),
        [(5 * devices, 128)],
        (exchange(modes), part_x, part_y, high, low),
        700000000,
        (
            pltpu.VMEM((2 * tiles * planes_z, 128), F32),
            pltpu.VMEM((2 * tiles * (planes_z + 2), 128), F32),
        ),
    )
    velocity, pressure = call(
        final_body,
        [(3, 1, rows, columns), (1, rows, columns)],
        (exchange(solved), u, later, high, low),
        500000000,
        (pltpu.VMEM((4, rows, columns), F32), pltpu.SemaphoreType.DMA((4,))),
        pl.ANY,
    )
    return velocity, pressure


def solution(mesh):
    return jax.shard_map(
        shards,
        mesh=mesh,
        in_specs=(
            P(None, "gz", "ma", None),
            P(None, "gz", "ma", None),
            P("gz", "ma", None),
            P("gz", "ma", None),
        ),
        out_specs=(P(None, "gz", "ma", None), P("gz", "ma", None)),
        check_vma=False,
    )
```

```python
import jax
import jax.numpy as jnp
import numpy as np
from jax import lax
from jax.experimental import pallas as pl
from jax.experimental.pallas import tpu as pltpu
from jax.sharding import PartitionSpec as P

SHIFT_TERM = 0.001
VISCOUS = 0.025
STRESS_LIQUID = 0.025
STRESS_GAS = 0.25
OLD_LIQUID = 0.225
VMEM_LIMIT = 16 * 1024 * 1024
F32 = jnp.float32
BF16 = jnp.bfloat16


def cosine_parts(count):
    index = np.arange(count, dtype=np.int64)
    product = index[:, None] * (2 * index[None, :] + 1) % (4 * count)
    angle = np.pi * product.astype(np.float64) / (2.0 * count)
    weight = np.where(index == 0, (1.0 / count) ** 0.5, (2.0 / count) ** 0.5)
    table = (weight[:, None] * np.cos(angle)).astype(np.float32)
    high = table.astype(BF16)
    low = (table - high.astype(np.float32)).astype(BF16)
    return high, low


def eigen_parts(count):
    index = np.arange(count).astype(np.float32)
    angle = np.float32(np.pi) * index / np.float32(count)
    return np.float32(2.0) - np.float32(2.0) * np.cos(angle).astype(np.float32)


def split(value):
    high = value.astype(BF16)
    return high, (value - high.astype(F32)).astype(BF16)


def product_3(a, b, dims):
    def dot(x, y):
        return lax.dot_general(x, y, (dims, ((), ())), preferred_element_type=F32)

    return dot(a[0], b[0]) + (dot(a[0], b[1]) + dot(a[1], b[0]))


def whole():
    return pl.BlockSpec(memory_space=pltpu.VMEM)


def call(body, outs, args, flops, scratch=(), out_space=pltpu.VMEM):
    shapes = [jax.ShapeDtypeStruct(shape, F32) for shape in outs]
    moved = sum(a.size * a.dtype.itemsize for a in args) + sum(4 * s.size for s in shapes)
    return pl.pallas_call(
        body,
        out_shape=shapes,
        in_specs=[whole() for _ in args],
        out_specs=[pl.BlockSpec(memory_space=out_space) for _ in outs],
        scratch_shapes=list(scratch),
        cost_estimate=pl.CostEstimate(flops=flops, bytes_accessed=moved, transcendentals=0),
        compiler_params=pltpu.CompilerParams(vmem_limit_bytes=VMEM_LIMIT),
    )(*args)


def near_sign():
    return jnp.where(lax.axis_index("gz") % 2 == 1, F32(1), F32(-1))


def rows_body(pred, stress, old, even_row, odd_row):
    rows = old.shape[1]
    even = lax.axis_index("ma") % 2 == 0

    planes = [pred.at[i, 0] for i in range(3)] + [stress.at[i, 0] for i in (0, 3, 4)] + [old.at[0]]
    for i, plane in enumerate(planes):
        low, high = plane[0:1], plane[rows - 1 : rows]
        even_row[i : i + 1] = jnp.where(even, high, low)
        odd_row[i : i + 1] = jnp.where(even, low, high)
    even_row[7:8] = jnp.zeros_like(even_row[7:8])
    odd_row[7:8] = jnp.zeros_like(odd_row[7:8])


def shifted(value, low_row=None, high_row=None):
    rows = value.shape[0]
    spot = lax.broadcasted_iota(jnp.int32, value.shape, 0)
    low_row = F32(0) if low_row is None else low_row
    high_row = F32(0) if high_row is None else high_row
    below = jnp.where(spot == 0, low_row, pltpu.roll(value, 1, 0))
    above = jnp.where(spot == rows - 1, high_row, pltpu.roll(value, rows - 1, 0))
    return below, above


def shifted_y(value):
    columns = value.shape[1]
    spot = lax.broadcasted_iota(jnp.int32, value.shape, 1)
    below = jnp.where(spot == 0, 0.0, pltpu.roll(value, 1, 1))
    above = jnp.where(spot == columns - 1, 0.0, pltpu.roll(value, columns - 1, 1))
    return below, above


def for_far(pred, stress, phase):
    sign = -near_sign()
    half = jnp.where(phase[0] == 1, sign * STRESS_LIQUID, sign * STRESS_GAS)
    add_x = VISCOUS * pred[0, 0] + half * stress[4, 0]
    return add_x, VISCOUS * pred[1, 0] + half * stress[5, 0]


def send_body(pred, stress, old, phase, _, far, near):
    rows = old.shape[1]
    sign = -near_sign()
    add_x, add_y = for_far(pred, stress, phase)
    behind, ahead = shifted(add_x)
    left, right = shifted_y(add_y)
    far[0:rows] = (ahead - behind) + (right - left)
    liquid = sign * (STRESS_LIQUID * stress[2, 0] + OLD_LIQUID * old[0])
    gas = (sign * STRESS_GAS) * stress[2, 0]
    viscous = VISCOUS * pred[2, 0]
    far[rows : 2 * rows] = viscous + jnp.where(phase[0] == 1, liquid, gas)
    far[2 * rows : 2 * rows + 1] = add_x[0:1]
    far[2 * rows + 1 : 2 * rows + 2] = add_x[rows - 1 : rows]
    far[2 * rows + 2 : 2 * rows + 8] = jnp.zeros((6, old.shape[2]), F32)
    near[0] = VISCOUS * pred[0, 0]
    near[1] = -sign * stress[4, 0]
    near[2] = VISCOUS * pred[1, 0]
    near[3] = -sign * stress[5, 0]
    near[4] = viscous - liquid
    near[5] = viscous - gas


def local_body(pred, stress, phase, old, even_row, odd_row, far_phase, out, later):
    later[0], later[1] = for_far(pred, stress, far_phase)
    even = lax.axis_index("ma") % 2 == 0
    before = jnp.where(even, odd_row[...], even_row[...])
    after = jnp.where(even, even_row[...], odd_row[...])
    liquid = phase[0] == 1
    half = jnp.where(liquid, STRESS_LIQUID, STRESS_GAS)

    def along_x(value, row):
        below, above = shifted(value, before[row : row + 1], after[row : row + 1])
        return above - below

    def along_y(value):
        below, above = shifted_y(value)
        return above - below

    for i in range(3):
        centre = pred[i, 0]
        below, above = shifted(centre, before[i : i + 1], after[i : i + 1])
        left, right = shifted_y(centre)
        total = centre + VISCOUS * ((below + above) + (left + right) - 6.0 * centre)
        if i == 0:
            force = along_x(stress[0, 0], 3) + along_y(stress[3, 0])
            push = along_x(old[0], 6)
        elif i == 1:
            force = along_x(stress[3, 0], 4) + along_y(stress[1, 0])
            push = along_y(old[0])
        else:
            force = along_x(stress[4, 0], 5) + along_y(stress[5, 0])
            push = None
        total = total + half * force
        if push is not None:
            total = total + jnp.where(liquid, OLD_LIQUID * push, 0.0)
        out[i] = total


def source_body(local, far, near, phase, high, low, out, sent):
    liquid = phase[0] == 1
    half = jnp.where(liquid, STRESS_LIQUID, STRESS_GAS)
    rows = local.shape[1]
    u_x = local[0] + (near[0] + half * near[1])
    u_y = local[1] + (near[2] + half * near[3])
    u_z = local[2] + far[rows : 2 * rows] + jnp.where(liquid, near[4], near[5])
    out[0], out[1], out[2] = u_x, u_y, u_z
    behind, ahead = shifted(u_x)
    left, right = shifted_y(u_y)
    planar = (ahead - behind) + (right - left) + far[0:rows]
    spot = lax.broadcasted_iota(jnp.int32, u_x.shape, 0)
    first = u_x[0:1] + far[2 * rows : 2 * rows + 1]
    last = u_x[rows - 1 : rows] + far[2 * rows + 1 : 2 * rows + 2]
    ends = jnp.where(spot == 0, first, jnp.where(spot == 1, last, 0.0))
    fields = split(jnp.concatenate([planar, u_z, ends], 0))
    modes = product_3((high[...], low[...]), fields, ((1,), (1,)))
    pairs = sent.shape[0] // 5
    for i in range(2):
        for j in range(2):
            sent[pl.ds(2 * i + j, pairs, 5)] = modes[
                j * pairs : (j + 1) * pairs, i * rows : (i + 1) * rows
            ]
    ends = modes[:, 2 * rows : 3 * rows]
    sent[pl.ds(4, pairs, 5)] = ends[:pairs] + pltpu.roll(ends[pairs:], 2, 1)


def solve_body(blocks, received, part_x, part_y, high, low, sent, held, result):
    planes = received.shape[0] // (5 * blocks)
    step = 5 * blocks
    tiles = part_x.shape[0] // 2
    lane = lax.broadcasted_iota(jnp.int32, (planes, 128), 1)
    row = lax.broadcasted_iota(jnp.int32, (planes, 128), 0)
    own = lax.axis_index("gz") * blocks + lax.axis_index("ma")
    mine = lax.broadcasted_iota(jnp.int32, part_y.shape, 1) == own
    wave_y = jnp.sum(jnp.where(mine, part_y[...], 0.0), axis=1, keepdims=True)
    spread = SHIFT_TERM + part_x[...] + wave_y
    r = 2.0 / (2.0 + spread + jnp.sqrt(spread * (spread + 4.0)))
    ends = [received[pl.ds(5 * b + 4, planes, step)] for b in range(blocks)]
    sides = []
    for j in range(2):
        parts = []
        for b in range(blocks):
            source = received[pl.ds(5 * b + j, planes, step)]
            if b + 1 < blocks:
                source = source + jnp.where(lane == 127, ends[b + 1][:, 2 * j : 2 * j + 1], 0.0)
            if b > 0:
                source = source - jnp.where(lane == 0, ends[b - 1][:, 2 * j + 1 : 2 * j + 2], 0.0)
            u_z = received[pl.ds(5 * b + 2 + j, planes, step)]
            up = jnp.where(row == planes - 1, 0.0, pltpu.roll(u_z, planes - 1, 0))
            down = jnp.where(row == 0, 0.0, pltpu.roll(u_z, 1, 0))
            parts.append(source + (up - down))
        sides.append(jnp.concatenate(parts, 1))
    table = (high[...], low[...])
    modes = product_3(split(jnp.concatenate(sides, 0)), table, ((1,), (1,)))
    every = 2 * tiles
    for j in range(2):
        for t in range(tiles):
            held[pl.ds(j * tiles + t, planes, every)] = modes[
                j * planes : (j + 1) * planes, t * 128 : (t + 1) * 128
            ]
    carry = jnp.zeros_like(r)
    for z in range(planes):
        carry = r * (carry - held[every * z : every * (z + 1)])
        held[every * z : every * (z + 1)] = carry
    carry = jnp.zeros_like(r)
    result[0:every] = carry
    result[every * (planes + 1) : every * (planes + 2)] = carry
    for z in reversed(range(planes)):
        carry = r * carry + held[every * z : every * (z + 1)]
        result[every * (z + 1) : every * (z + 2)] = carry
    fields = []
    for j in range(2):
        pieces = [result[pl.ds(every + j * tiles + t, planes, every)] for t in range(tiles)]
        fields.append(jnp.concatenate(pieces, 1))
    for j in range(2):
        pieces = [
            result[pl.ds(2 * every + j * tiles + t, planes, every)]
            - result[pl.ds(j * tiles + t, planes, every)]
            for t in range(tiles)
        ]
        fields.append(jnp.concatenate(pieces, 1))
    back = product_3(split(jnp.concatenate(fields, 0)), table, ((1,), (0,)))
    for i in range(4):
        for b in range(blocks):
            sent[pl.ds(5 * b + i, planes, step)] = back[
                i * planes : (i + 1) * planes, b * 128 : (b + 1) * 128
            ]
    for b in range(blocks):
        edge = jnp.zeros((planes, 128), F32)
        for j in range(2):
            mine = back[j * planes : (j + 1) * planes]
            if b > 0:
                edge = jnp.where(lane == 2 * j, mine[:, b * 128 - 1 : b * 128], edge)
            if b + 1 < blocks:
                edge = jnp.where(
                    lane == 2 * j + 1, mine[:, b * 128 + 128 : b * 128 + 129], edge
                )
        sent[pl.ds(5 * b + 4, planes, step)] = edge


def whole_body(u, later, out):
    out[0] = u[0] + later[0]
    out[1] = u[1] + later[1]
    out[2] = u[2]


def final_body(received, u, high, low, velocity, pressure, made, arrived):
    pairs = received.shape[0] // 5
    table = (high[...], low[...])
    nn = ((1,), (0,))
    places = (velocity.at[0, 0], velocity.at[1, 0], velocity.at[2, 0], pressure.at[0])
    copies = [pltpu.make_async_copy(made.at[i], places[i], arrived.at[i]) for i in range(4)]

    def field(i):
        pieces = [received[pl.ds(i + j, pairs, 5)] for j in range(2)]
        return product_3(split(jnp.concatenate(pieces, 0).T), table, nn)

    made[2] = u[2] - 0.25 * field(2)
    copies[2].start()
    p = field(0)
    made[3] = p
    copies[3].start()
    left, right = shifted_y(p)
    made[1] = u[1] - 0.25 * (right - left)
    copies[1].start()
    ends = split(received[pl.ds(4, pairs, 5)].T[0:8])
    lead = product_3(ends, (high[:pairs], low[:pairs]), nn)
    trail = product_3(ends, (high[pairs:], low[pairs:]), nn)
    behind, ahead = shifted(p, lead[0:1] + trail[2:3], lead[1:2] + trail[3:4])
    made[0] = u[0] - 0.25 * (ahead - behind)
    copies[0].start()
    for copy in copies:
        copy.wait()


def shards(predictor, stress, phase, old_pressure):
    planes_z, lines = lax.axis_size("gz"), lax.axis_size("ma")
    rows, columns = old_pressure.shape[1], old_pressure.shape[2]
    devices = planes_z * lines
    table = cosine_parts(columns)
    high, low = jnp.asarray(table[0]), jnp.asarray(table[1])
    eigen = eigen_parts(columns)

    def swap(value, axis, begin):
        pairs = [(i, i + 1) for i in range(begin, lax.axis_size(axis) - 1, 2)]
        return lax.ppermute(value, axis, pairs + [(b, a) for a, b in pairs])

    far_phase = swap(phase, "gz", 1)
    even_row, odd_row = call(
        rows_body, [(8, columns), (8, columns)], (predictor, stress, old_pressure), 10000
    )
    far, near = call(
        send_body,
        [(2 * rows + 8, columns), (6, rows, columns)],
        (predictor, stress, old_pressure, far_phase, even_row),
        1000000,
    )
    far = swap(far, "gz", 1)
    near = swap(near, "gz", 0)
    even_row = swap(even_row, "ma", 0)
    odd_row = swap(odd_row, "ma", 1)

    local, later = call(
        local_body,
        [(3, rows, columns), (2, rows, columns)],
        (predictor, stress, phase, old_pressure, even_row, odd_row, far_phase),
        8000000,
    )
    later = swap(later, "gz", 1)
    u, modes = call(
        source_body,
        [(3, rows, columns), (5 * devices, 128)],
        (local, far, near, phase, high, low),
        600000000,
    )

    def exchange(value):
        count = value.shape[0]
        moved = lax.all_to_all(value.reshape(count, 1, 128), ("gz", "ma"), 0, 0, tiled=True)
        return moved.reshape(count, 128)

    tiles = columns // 128
    part_x = jnp.asarray(np.tile(eigen.reshape(tiles, 128), (2, 1)))
    part_y = jnp.asarray(np.repeat(eigen.reshape(2, devices), tiles, axis=0))
    (solved,) = call(
        lambda *refs: solve_body(lines, *refs),
        [(5 * devices, 128)],
        (exchange(modes), part_x, part_y, high, low),
        20000000000,
        (
            pltpu.VMEM((2 * tiles * planes_z, 128), F32),
            pltpu.VMEM((2 * tiles * (planes_z + 2), 128), F32),
        ),
    )
    (u,) = call(whole_body, [(3, rows, columns)], (u, later), 20000000000)
    velocity, pressure = call(
        final_body,
        [(3, 1, rows, columns), (1, rows, columns)],
        (exchange(solved), u, high, low),
        500000000,
        (pltpu.VMEM((4, rows, columns), F32), pltpu.SemaphoreType.DMA((4,))),
        pl.ANY,
    )
    return velocity, pressure


def solution(mesh):
    return jax.shard_map(
        shards,
        mesh=mesh,
        in_specs=(
            P(None, "gz", "ma", None),
            P(None, "gz", "ma", None),
            P("gz", "ma", None),
            P("gz", "ma", None),
        ),
        out_specs=(P(None, "gz", "ma", None), P("gz", "ma", None)),
        check_vma=False,
    )
```
